256 devices in a mesh: train: 32 (over z_lo, y, core), task: 8 (over x, z_hi).
Axes of the slice: x: 4, y: 4, z: 8 (z_hi: 2, z_lo: 4; z = z_hi * 4 + z_lo), core: 2. Of those that a mesh axis runs over, the one named last changes fastest.
Arguments:
- train_grads: bfloat16 [1048576, 1024], P(('train', 'task')), may hold values from -6 to 6
- queries: bfloat16 [4096, 1024], P(('task', 'train')), may hold values from -6 to 6
- pair_blocks: int32 [4096, 4], P(('train', 'task')), may hold values from 0 to 31
- counts: int32 [4096], P(('train', 'task')), may hold values from 1 to 4, as said below
Outputs:
- scores: bfloat16 [4096, 4, 256, 128], P(('train', 'task'))
The draws below stay inside these ranges and needn't reach their ends.
Inputs may be any that keep to these rules, and one draw needn't show every extreme that they name: `counts`: some train block has all 4 slots live.
All inputs are finite; a program needn't handle non-finite values.
Results may differ from the reference program's by a relative error of at most 0.002.
The reference program's roundings to bfloat16 on the way (of `precond`) count: a program that leaves them out, or rounds other values in their place, can miss the bound.
Values may be sent and summed in bfloat16 or wider, within the bound.
A program may use at most 128 MiB of HBM per device.

```python
import math
import jax
import jax.numpy as jnp
from jax import lax

K = 1024
TRB = 256
QROWS = 128
SLOTS = 4
NTRAIN = 1048576
NBLK = 4096
QUERIES = 4096
TASK_BLOCKS = 32


def draw_counts(key, part):
    key = jax.random.fold_in(key, 7)
    first_key, second_key = jax.random.split(key)
    values = jax.random.randint(first_key, (NBLK,), 1, SLOTS + 1)
    position = jax.random.randint(second_key, (), 0, NBLK)
    return values.at[position].set(SLOTS).astype(jnp.int32)


def with_ends(result, stream_key, low, largest):
    place = [jax.random.randint(jax.random.fold_in(stream_key, axis), (), 0, length) for axis, length in enumerate(result.shape)]
    longest = result.shape.index(max(result.shape))
    neighbour = place[:longest] + [(place[longest] + 1) % result.shape[longest]] + place[longest + 1:]
    return result.at[tuple(place)].set(low).at[tuple(neighbour)].set(largest)


def levels(own_key, dims, cuts, least, largest):
    gain, own = 1.0, jax.random.fold_in(own_key, 6)
    for axis_at, blocks in cuts:
        heights = jnp.exp(jax.random.uniform(jax.random.fold_in(own, axis_at), (blocks,), jnp.float32, least / len(cuts), largest / len(cuts)))
        gain = gain * jnp.repeat(heights, dims[axis_at] // blocks).reshape([-1 if axis == axis_at else 1 for axis in range(len(dims))])
    return gain


def normal_values(own_key, dims, width, reach, pieces=(), kind=jnp.bfloat16):
    result = jax.random.normal(own_key, dims, jnp.float32) * width
    if len(pieces) > 0:
        result = levels(own_key, dims, pieces, -0.22, 0.18) * result
    return jnp.clip(result, min=-reach, max=reach).astype(kind)


def setup_inputs(seed: int = 0) -> dict:
    keys = jax.random.split(jax.random.key(seed), 5)
    return {
        "train_grads": normal_values(keys[0], (NTRAIN, K), 1.0, 6.0, ((0, 256),)),
        "queries": normal_values(keys[1], (QUERIES, K), 1.0, 6.0, ((0, 256),)),
        "pair_blocks": with_ends(jax.random.randint(keys[2], (NBLK, SLOTS), 0, TASK_BLOCKS), jax.random.fold_in(keys[2], 1), 0, TASK_BLOCKS - 1).astype(jnp.int32),
        "counts": draw_counts(jax.random.fold_in(keys[4], 71), 0),
    }


def reference(train_grads, queries, pair_blocks, counts):
    gram = jnp.dot(train_grads.T.astype(jnp.float32), train_grads.astype(jnp.float32), preferred_element_type=jnp.float32)
    fisher = gram / NTRAIN + 0.1 * jnp.eye(K, dtype=jnp.float32)
    factor = jnp.linalg.cholesky(fisher)
    half_solved = lax.linalg.triangular_solve(factor, queries.astype(jnp.float32), left_side=False, lower=True, transpose_a=True)
    precond = lax.linalg.triangular_solve(factor, half_solved, left_side=False, lower=True).astype(jnp.bfloat16)
    task_blocks = precond.reshape(TASK_BLOCKS, QROWS, K)
    train_blocks = train_grads.reshape(NBLK, TRB, K)
    scale = 1.0 / math.sqrt(K)

    def score_block(inputs):
        grad_block, pair_row, live_count = inputs
        chosen = task_blocks[pair_row]
        values = jnp.einsum('tk,sqk->stq', grad_block.astype(jnp.float32), chosen.astype(jnp.float32)) * scale
        live_slots = jnp.arange(SLOTS, dtype=jnp.int32) < live_count
        return jnp.where(live_slots[:, None, None], values, 0.0).astype(jnp.bfloat16)
    return lax.map(score_block, (train_blocks, pair_blocks, counts))
```

```python
import functools
import math

import jax
import jax.numpy as jnp
from jax import lax
from jax.experimental import pallas as pl
from jax.experimental.pallas import tpu as pltpu
from jax.sharding import PartitionSpec as P

MESH = pl.DeviceIdType.MESH
TRB = 256
QROWS = 128
BLK = 128
NB = 8
DAMP = 0.1
TAU = 1e-5
PAIRS = [(i, j) for i in range(NB) for j in range(i + 1)]
SLOT = {pair: n for n, pair in enumerate(PAIRS)}
VMEM_LIMIT = 56 * 1024 * 1024


def coords():
    t, k = lax.axis_index("train"), lax.axis_index("task")
    core, y, x = lax.rem(t, 2), lax.rem(t // 2, 4), k // 2
    z = lax.rem(k, 2) * 4 + t // 8
    return core, x, y, z


def device(core, x, y, z):
    return ((lax.rem(z, 4) * 4 + y) * 2 + core, x * 2 + z // 4)


def meet(peers):
    barrier = pltpu.get_barrier_semaphore()
    for peer in peers:
        pl.semaphore_signal(barrier, inc=1, device_id=peer, device_id_type=MESH)
    pl.semaphore_wait(barrier, len(peers))


def gram_kernel(t_ref, out_ref):
    first = pl.program_id(0) == 0

    @pl.when(first)
    def _():
        out_ref[...] = jnp.zeros_like(out_ref)

    for bi in range(NB // 2):
        for bj in range(bi + 1):
            part = lax.dot_general(
                t_ref[:, bi * 256:(bi + 1) * 256],
                t_ref[:, bj * 256:(bj + 1) * 256],
                (((0,), (0,)), ((), ())),
                preferred_element_type=jnp.float32,
            )
            for u in range(2):
                for v in range(2):
                    pair = (2 * bi + u, 2 * bj + v)
                    if pair in SLOT:
                        at = SLOT[pair] * BLK
                        out_ref[at:at + BLK, :] += part[u * BLK:(u + 1) * BLK, v * BLK:(v + 1) * BLK]


def local_gram(t):
    rows, width = t.shape
    step = 1024
    return pl.pallas_call(
        gram_kernel,
        grid=(rows // step,),
        in_specs=[pl.BlockSpec((step, width), lambda i: (i, 0))],
        out_specs=pl.BlockSpec((len(PAIRS) * BLK, BLK), lambda i: (0, 0)),
        out_shape=jax.ShapeDtypeStruct((len(PAIRS) * BLK, BLK), jnp.float32),
        compiler_params=pltpu.CompilerParams(vmem_limit_bytes=VMEM_LIMIT),
        name="local_gram",
    )(t)


ROWS = 72
ZROWS = 24


def sum_kernel(g_ref, out_ref, r0, s1, ra, s2, rb, s3, rz, fz, send, recv):
    core, x, y, z = coords()
    sibling = device(1 - core, x, y, z)

    def along(axis, d):
        if axis == 0:
            return device(core, lax.rem(x + d, 4), y, z)
        if axis == 1:
            return device(core, x, lax.rem(y + d, 4), z)
        return device(core, x, y, lax.rem(z + d, 8))

    meet([sibling] + [along(a, d) for a in (0, 1) for d in (1, 2, 3)] + [along(2, d) for d in range(1, 8)])
    count = [0]

    def start(src, dst, to):
        n = count[0]
        count[0] += 1
        copy = pltpu.make_async_remote_copy(
            src_ref=src, dst_ref=dst, send_sem=send.at[n], recv_sem=recv.at[n], device_id=to, device_id_type=MESH
        )
        copy.start()
        return copy

    me = (x, y)
    copy = start(g_ref.at[1 - core], r0, sibling)
    copy.wait()
    s1[...] = g_ref[core] + r0[...]
    copies = []
    for h in range(2):
        for d in (1, 2, 3):
            copies.append(start(s1.at[h, lax.rem(me[h] + d, 4)], ra.at[h, d - 1], along(h, d)))
    for copy in copies:
        copy.wait()
    for h in range(2):
        s2[h] = s1[h, me[h]] + ra[h, 0] + ra[h, 1] + ra[h, 2]
    copies = []
    for h in range(2):
        for d in (1, 2, 3):
            copies.append(start(s2.at[h, lax.rem(me[1 - h] + d, 4)], rb.at[h, d - 1], along(1 - h, d)))
    for copy in copies:
        copy.wait()
    for h in range(2):
        s3[h * ROWS:(h + 1) * ROWS, :] = s2[h, me[1 - h]] + rb[h, 0] + rb[h, 1] + rb[h, 2]
    s3[2 * ROWS:, :] = jnp.zeros((8 * ZROWS - 2 * ROWS, BLK), jnp.float32)
    copies = []
    for d in range(1, 8):
        at = pl.multiple_of(lax.rem(z + d, 8) * ZROWS, 8)
        copies.append(start(s3.at[pl.ds(at, ZROWS)], rz.at[d - 1], along(2, d)))
    for copy in copies:
        copy.wait()
    mine = pl.ds(pl.multiple_of(z * ZROWS, 8), ZROWS)
    total = s3[mine, :]
    for d in range(7):
        total += rz[d]
    fz[mine, :] = total
    copies = [start(fz.at[mine], fz.at[mine], along(2, d)) for d in range(1, 8)]
    for copy in copies:
        copy.wait()
    out_ref[core, 0, x, y] = fz[0:ROWS, :]
    out_ref[core, 1, y, x] = fz[ROWS:2 * ROWS, :]
    copies = []
    for h in range(2):
        piece = out_ref.at[core, h, me[h], me[1 - h]]
        for d in (1, 2, 3):
            copies.append(start(piece, piece, along(1 - h, d)))
    for copy in copies:
        copy.wait()
    copies = []
    for h in range(2):
        piece = out_ref.at[core, h, me[h]]
        for d in (1, 2, 3):
            copies.append(start(piece, piece, along(h, d)))
    for copy in copies:
        copy.wait()
    copy = start(out_ref.at[core], out_ref.at[core], sibling)
    copy.wait()


def sum_gram(packed):
    shape = (2, 2, 4, 4, ROWS, BLK)
    f32 = jnp.float32
    out = pl.pallas_call(
        sum_kernel,
        in_specs=[pl.BlockSpec(memory_space=pltpu.VMEM)],
        out_specs=pl.BlockSpec(memory_space=pltpu.VMEM),
        out_shape=jax.ShapeDtypeStruct(shape, f32),
        scratch_shapes=[
            pltpu.VMEM(shape[1:], f32),
            pltpu.VMEM(shape[1:], f32),
            pltpu.VMEM((2, 3, 4, ROWS, BLK), f32),
            pltpu.VMEM((2, 4, ROWS, BLK), f32),
            pltpu.VMEM((2, 3, ROWS, BLK), f32),
            pltpu.VMEM((8 * ZROWS, BLK), f32),
            pltpu.VMEM((7, ZROWS, BLK), f32),
            pltpu.VMEM((8 * ZROWS, BLK), f32),
            pltpu.SemaphoreType.DMA((40,)),
            pltpu.SemaphoreType.DMA((40,)),
        ],
        compiler_params=pltpu.CompilerParams(collective_id=0, has_side_effects=True, vmem_limit_bytes=VMEM_LIMIT),
        name="sum_gram",
    )(packed.reshape(shape))
    return out.reshape(-1, BLK)


def split(v):
    hi = v.astype(jnp.bfloat16)
    return hi, (v - hi.astype(jnp.float32)).astype(jnp.bfloat16)


def solve_kernel(total, most, g_ref, q_ref, out_ref, flag_ref, hi_ref, lo_ref, d_ref):
    width = q_ref.shape[1]
    eye = lax.broadcasted_iota(jnp.int32, (BLK, BLK), 0) == lax.broadcasted_iota(jnp.int32, (BLK, BLK), 1)
    square = jnp.zeros((BLK, BLK), jnp.float32)
    for i, j in PAIRS:
        at = SLOT[i, j] * BLK
        block = g_ref[at:at + BLK, :] * (1.0 / total)
        if i == j:
            d_ref[:, i * BLK:(i + 1) * BLK] = jnp.sum(jnp.where(eye, block, 0.0), axis=0, keepdims=True) + DAMP
            block = jnp.where(eye, 0.0, block)
            square += block * block
        else:
            square += 2.0 * block * block
        hi, lo = split(block)
        hi_ref[i * BLK:(i + 1) * BLK, j * BLK:(j + 1) * BLK] = hi
        lo_ref[i * BLK:(i + 1) * BLK, j * BLK:(j + 1) * BLK] = lo
        if i != j:
            hi, lo = split(block.T)
            hi_ref[j * BLK:(j + 1) * BLK, i * BLK:(i + 1) * BLK] = hi
            lo_ref[j * BLK:(j + 1) * BLK, i * BLK:(i + 1) * BLK] = lo
    size = jnp.sum(square)
    diag = d_ref[...]
    rows = q_ref.shape[0]

    def apply(v):
        hi, lo = split(v)
        both = jnp.dot(jnp.concatenate([hi, lo], axis=0), hi_ref[...], preferred_element_type=jnp.float32)
        low = jnp.dot(hi, lo_ref[...], preferred_element_type=jnp.float32)
        return v * diag + (both[:rows] + (both[rows:] + low))

    def dots(a, b):
        return jnp.sum(a * b, axis=1, keepdims=True)

    def unsolved(state):
        step, _, _, _, _, left = state
        return jnp.logical_and(step < most, left > 0.0)

    def advance(state):
        step, sol, res, way, rr, _ = state
        image = apply(way)
        bend = dots(way, image)
        alpha = jnp.where(bend > 0.0, rr / bend, 0.0)
        sol = sol + alpha * way
        res = res - alpha * image
        after = dots(res, res)
        beta = jnp.where(rr > 0.0, after / rr, 0.0)
        left = jnp.sum(jnp.where(after <= (DAMP * TAU) ** 2 * dots(sol, sol), 0.0, 1.0))
        return step + 1, sol, res, res + beta * way, after, left

    res = q_ref[...].astype(jnp.float32)
    state = (jnp.int32(0), jnp.zeros((rows, width), jnp.float32), res, res, dots(res, res), jnp.float32(1.0))
    _, sol, _, _, _, left = lax.while_loop(unsolved, advance, state)
    out_ref[...] = sol.astype(jnp.bfloat16)
    good = jnp.logical_and(left == 0.0, size <= 4.0)
    flag_ref[0, 0] = jnp.where(good, 1, 0).astype(jnp.int32)


def solve(packed, queries, total):
    rows, width = queries.shape
    return pl.pallas_call(
        functools.partial(solve_kernel, total, 48),
        in_specs=[pl.BlockSpec(memory_space=pltpu.VMEM)] * 2,
        out_specs=[pl.BlockSpec(memory_space=pltpu.VMEM), pl.BlockSpec(memory_space=pltpu.SMEM)],
        out_shape=[
            jax.ShapeDtypeStruct((rows, width), jnp.bfloat16),
            jax.ShapeDtypeStruct((1, 1), jnp.int32),
        ],
        scratch_shapes=[
            pltpu.VMEM((width, width), jnp.bfloat16),
            pltpu.VMEM((width, width), jnp.bfloat16),
            pltpu.VMEM((1, width), jnp.float32),
        ],
        compiler_params=pltpu.CompilerParams(vmem_limit_bytes=VMEM_LIMIT),
        name="solve_rows",
    )(packed, queries)


def solve_direct(packed, queries, total):
    width = queries.shape[1]
    blocks = packed.reshape(len(PAIRS), BLK, BLK)
    rows = []
    for i in range(NB):
        row = [blocks[SLOT[i, j]] if i >= j else blocks[SLOT[j, i]].T for j in range(NB)]
        rows.append(jnp.concatenate(row, axis=1))
    fisher = jnp.concatenate(rows, axis=0) / total + DAMP * jnp.eye(width, dtype=jnp.float32)
    factor = jnp.linalg.cholesky(fisher)
    half = lax.linalg.triangular_solve(
        factor, queries.astype(jnp.float32), left_side=False, lower=True, transpose_a=True
    )
    return lax.linalg.triangular_solve(factor, half, left_side=False, lower=True).astype(jnp.bfloat16)


def gather_kernel(p_ref, out_ref, send, recv, own_sem):
    core, x, y, z = coords()
    sibling = device(1 - core, x, y, z)

    def along(axis, d):
        if axis == 0:
            return device(core, lax.rem(x + d, 4), y, z)
        if axis == 1:
            return device(core, x, lax.rem(y + d, 4), z)
        return device(core, x, y, lax.rem(z + d, 8))

    meet([sibling] + [along(a, d) for a in (0, 1) for d in (1, 3)] + [along(2, d) for d in range(1, 8)])
    count = [0]

    def start(piece, to, src=None):
        n = count[0]
        count[0] += 1
        copy = pltpu.make_async_remote_copy(
            src_ref=piece if src is None else src,
            dst_ref=piece,
            send_sem=send.at[n],
            recv_sem=recv.at[n],
            device_id=to,
            device_id_type=MESH,
        )
        copy.start()
        return copy

    me = (x, y)
    home = out_ref.at[:, x, z, y, core]
    own = pltpu.make_async_copy(p_ref, home, own_sem)
    own.start()
    copies = [start(home, along(2, d), p_ref) for d in range(1, 8)]
    own.wait()
    for copy in copies:
        copy.wait()

    def second(h, v, zs):
        if h == 0:
            return out_ref.at[0, x, zs, lax.rem(v, 4), core]
        return out_ref.at[1, lax.rem(v, 4), zs, y, core]

    def first(h, v, zs):
        if h == 0:
            return out_ref.at[0, lax.rem(v, 4), zs, :, core]
        return out_ref.at[1, :, zs, lax.rem(v, 4), core]

    whole, low, high = pl.ds(0, 8), pl.ds(0, 4), pl.ds(4, 4)
    copies = []
    for h in range(2):
        piece = second(h, me[1 - h], whole)
        copies += [start(piece, along(1 - h, 1)), start(piece, along(1 - h, 3))]
    for copy in copies:
        copy.wait()
    copies = []
    for h in range(2):
        copies.append(start(second(h, me[1 - h] + 3, low), along(1 - h, 1)))
        copies.append(start(second(h, me[1 - h] + 1, high), along(1 - h, 3)))
    for copy in copies:
        copy.wait()
    copies, over = [], []
    for h in range(2):
        piece = first(h, me[h], whole)
        copies += [start(piece, along(h, 1)), start(piece, along(h, 3))]
        over.append(start(piece, sibling))
    for copy in copies:
        copy.wait()
    copies = []
    for h in range(2):
        copies.append(start(first(h, me[h] + 3, low), along(h, 1)))
        copies.append(start(first(h, me[h] + 1, high), along(h, 3)))
        over.append(start(first(h, me[h] + 3, whole), sibling))
        over.append(start(first(h, me[h] + 1, whole), sibling))
    for copy in copies:
        copy.wait()
    for h in range(2):
        over.append(start(first(h, me[h] + 2, whole), sibling))
    for copy in over:
        copy.wait()


def gather_queries(precond):
    rows, width = precond.shape
    halves = precond.reshape(rows, 2, width // 2).transpose(1, 0, 2)
    out = pl.pallas_call(
        gather_kernel,
        in_specs=[pl.BlockSpec(memory_space=pltpu.VMEM)],
        out_specs=pl.BlockSpec(memory_space=pl.ANY),
        out_shape=jax.ShapeDtypeStruct((2, 4, 8, 4, 2, rows, width // 2), jnp.bfloat16),
        scratch_shapes=[
            pltpu.SemaphoreType.DMA((40,)),
            pltpu.SemaphoreType.DMA((40,)),
            pltpu.SemaphoreType.DMA,
        ],
        compiler_params=pltpu.CompilerParams(collective_id=1, has_side_effects=True, vmem_limit_bytes=VMEM_LIMIT),
        name="gather_queries",
    )(halves)
    return out.reshape(2, 32, QROWS, width // 2)


def score_kernel(scale, pair_ref, count_ref, t_ref, p_ref, out_ref):
    b = pl.program_id(0)
    half = t_ref.shape[1] // 2
    nt = (((1,), (1,)), ((), ()))
    for s in range(out_ref.shape[1]):
        live = s < count_ref[b]

        @pl.when(live)
        def _():
            q = pair_ref[b * out_ref.shape[1] + s]
            value = lax.dot_general(t_ref[:, :half], p_ref[0, q], nt, preferred_element_type=jnp.float32)
            value += lax.dot_general(t_ref[:, half:], p_ref[1, q], nt, preferred_element_type=jnp.float32)
            out_ref[0, s] = (value * scale).astype(out_ref.dtype)

        @pl.when(jnp.logical_not(live))
        def _():
            out_ref[0, s] = jnp.zeros(out_ref.shape[2:], out_ref.dtype)


def score(t, queries, pair_blocks, counts):
    blocks, slots = pair_blocks.shape
    width = t.shape[1]
    return pl.pallas_call(
        functools.partial(score_kernel, 1.0 / math.sqrt(width)),
        grid_spec=pltpu.PrefetchScalarGridSpec(
            num_scalar_prefetch=2,
            grid=(blocks,),
            in_specs=[
                pl.BlockSpec((TRB, width), lambda b, *_: (b, 0)),
                pl.BlockSpec(queries.shape, lambda b, *_: (0, 0, 0, 0), pipeline_mode=pl.Buffered(1)),
            ],
            out_specs=pl.BlockSpec((1, slots, TRB, QROWS), lambda b, *_: (b, 0, 0, 0)),
        ),
        out_shape=jax.ShapeDtypeStruct((blocks, slots, TRB, QROWS), jnp.bfloat16),
        compiler_params=pltpu.CompilerParams(vmem_limit_bytes=VMEM_LIMIT),
        name="scores",
    )(pair_blocks.reshape(-1), counts, t, queries)


def per_device(train_grads, queries, pair_blocks, counts):
    total = lax.axis_size("train") * lax.axis_size("task") * train_grads.shape[0]
    packed = sum_gram(local_gram(train_grads))
    precond, flag = solve(packed, queries, total)
    precond = lax.cond(
        flag[0, 0] > 0,
        lambda p, g, q: p,
        lambda p, g, q: solve_direct(g, q, total),
        precond, packed, queries,
    )
    return score(train_grads, gather_queries(precond), pair_blocks, counts)


def solution(mesh):
    in_specs = (
        P(("train", "task"), None),
        P(("task", "train"), None),
        P(("train", "task"), None),
        P(("train", "task")),
    )
    out_specs = P(("train", "task"), None, None, None)
    return jax.shard_map(
        per_device, mesh=mesh, in_specs=in_specs, out_specs=out_specs, check_vma=False
    )
```

```python
import functools
import math

import jax
import jax.numpy as jnp
from jax import lax
from jax.experimental import pallas as pl
from jax.experimental.pallas import tpu as pltpu
from jax.sharding import PartitionSpec as P

MESH = pl.DeviceIdType.MESH
TRB = 256
QROWS = 128
BLK = 128
NB = 8
DAMP = 0.1
TAU = 1e-5
WIDE = 256


def coords():
    t, k = lax.axis_index("train"), lax.axis_index("task")
    core, y, x = lax.rem(t, 2), lax.rem(t // 2, 4), k // 2
    z = lax.rem(k, 2) * 4 + t // 8
    return core, x, y, z


def device(core, x, y, z):
    return ((lax.rem(z, 4) * 4 + y) * 2 + core, x * 2 + z // 4)


ROWS = 72
HALF = 32 * ROWS
ZROWS = 24


def wide_blocks(c):
    return [(2 * c, 2 * c), (2 * c + 1, 2 * c + 1), (2 * c + 1, 2 * c), (2 + c, 1 - c), (2 + c, c)]


def parts_of(n):
    return [(0, 0), (1, 0), (1, 1)] if n < 2 else [(0, 0), (0, 1), (1, 0), (1, 1)]


PAIRS = [(2 * i + u, 2 * j + v) for c in (0, 1) for n, (i, j) in enumerate(wide_blocks(c)) for u, v in parts_of(n)]
SLOT = {pair: n for n, pair in enumerate(PAIRS)}
SPANS = []
for index in range(5):
    begin = SPANS[-1][1] if SPANS else 0
    SPANS.append((begin, begin + BLK * len(parts_of(index))))


def gram_kernel(t_ref, q_ref, out_ref, qf_ref, qz_ref, tv, gs, r0, s1, ra, s2, rb, s3, rz, fz, t_sem, q_sem, send, recv):
    core, x, y, z = coords()
    other = 1 - core
    sibling = device(other, x, y, z)

    def along(axis, d):
        if axis == 0:
            return device(core, lax.rem(x + d, 4), y, z)
        if axis == 1:
            return device(core, x, lax.rem(y + d, 4), z)
        return device(core, x, y, lax.rem(z + d, 8))

    loads = []
    for n, panel in enumerate((2 * other, 2 * other + 1, 2 * core, 2 * core + 1)):
        column = pl.multiple_of(panel * WIDE, WIDE)
        loads.append(pltpu.make_async_copy(t_ref.at[:, pl.ds(column, WIDE)], tv.at[panel], t_sem.at[n]))
        loads[n].start()
    place = pl.ds(pl.multiple_of(z * q_ref.shape[0], 16), q_ref.shape[0])
    own_q = pltpu.make_async_copy(q_ref, qz_ref.at[place], q_sem)
    own_q.start()
    peers = [sibling] + [along(a, d) for a in (0, 1) for d in (1, 2, 3)] + [along(2, d) for d in range(1, 8)]
    barrier = pltpu.get_barrier_semaphore()
    for peer in peers:
        pl.semaphore_signal(barrier, inc=1, device_id=peer, device_id_type=MESH)
    count = [0]

    def start(src, dst, to):
        n = count[0]
        count[0] += 1
        copy = pltpu.make_async_remote_copy(
            src_ref=src, dst_ref=dst, send_sem=send.at[n], recv_sem=recv.at[n], device_id=to, device_id_type=MESH
        )
        copy.start()
        return copy

    def block(i, j):
        return lax.dot_general(
            tv[i], tv[j], (((0,), (0,)), ((), ())), preferred_element_type=jnp.float32
        )

    def pieces(n, value):
        for p, (u, v) in enumerate(parts_of(n)):
            at = SPANS[n][0] + p * BLK
            yield at, value[u * BLK:(u + 1) * BLK, v * BLK:(v + 1) * BLK]

    def rows(at, length):
        return pl.ds(pl.multiple_of(at, 8), length)

    me = (x, y)
    finish, cross = [], []
    for n, (i, j) in enumerate(wide_blocks(other)):
        if n < 2:
            loads[n].wait()
        elif n > 2:
            loads[n - 1].wait()
        value = block(i, j)
        for at, part in pieces(n, value):
            gs[at:at + BLK, :] = part
        if n == 0:
            pl.semaphore_wait(barrier, len(peers))
            finish += [start(q_ref, qz_ref.at[place], along(2, d)) for d in range(1, 8)]
        span = pl.ds(SPANS[n][0], SPANS[n][1] - SPANS[n][0])
        cross.append(start(gs.at[span], r0.at[span], sibling))

    def first_sends(h):
        out = []
        for d in (1, 2, 3):
            at = (h * 4 + lax.rem(me[h] + d, 4)) * 4 * ROWS
            out.append(start(s1.at[rows(at, 4 * ROWS)], ra.at[h, d - 1], along(h, d)))
        return out

    first = [None, None]
    for n, (i, j) in enumerate(wide_blocks(core)):
        value = block(i, j)
        cross[n].wait_recv()
        for at, part in pieces(n, value):
            s1[at:at + BLK, :] = part + r0[at:at + BLK, :]
        if n == 2:
            first[0] = first_sends(0)
    first[1] = first_sends(1)
    second = [None, None]
    for h in range(2):
        for copy in first[h]:
            copy.wait_recv()
        s2[h] = s1[rows((h * 4 + me[h]) * 4 * ROWS, 4 * ROWS), :] + ra[h, 0] + ra[h, 1] + ra[h, 2]
        second[h] = []
        for d in (1, 2, 3):
            at = lax.rem(me[1 - h] + d, 4) * ROWS
            second[h].append(start(s2.at[h, rows(at, ROWS)], rb.at[h, d - 1], along(1 - h, d)))
    s3[2 * ROWS:, :] = jnp.zeros((8 * ZROWS - 2 * ROWS, BLK), jnp.float32)
    for h in range(2):
        for copy in second[h]:
            copy.wait_recv()
        s3[h * ROWS:(h + 1) * ROWS, :] = s2[h, rows(me[1 - h] * ROWS, ROWS), :] + rb[h, 0] + rb[h, 1] + rb[h, 2]
    there = []
    for d in range(1, 8):
        there.append(start(s3.at[rows(lax.rem(z + d, 8) * ZROWS, ZROWS)], rz.at[d - 1], along(2, d)))
    for copy in there:
        copy.wait_recv()
    mine = rows(z * ZROWS, ZROWS)
    total = s3[mine, :]
    for d in range(7):
        total += rz[d]
    fz[mine, :] = total
    back = [start(fz.at[mine], fz.at[mine], along(2, d)) for d in range(1, 8)]
    for copy in back:
        copy.wait_recv()
    base = core * HALF

    def chunk(h, a):
        return out_ref.at[rows(base + (h * 4 + a) * 4 * ROWS, 4 * ROWS)]

    spread = [[], []]
    for h in range(2):
        at = rows(base + ((h * 4 + me[h]) * 4 + me[1 - h]) * ROWS, ROWS)
        out_ref[at, :] = fz[h * ROWS:(h + 1) * ROWS, :]
        for d in (1, 2, 3):
            spread[h].append(start(out_ref.at[at], out_ref.at[at], along(1 - h, d)))
    wide, over = [[], []], []
    for h in range(2):
        for copy in spread[h]:
            copy.wait_recv()
        piece = chunk(h, me[h])
        for d in (1, 2, 3):
            wide[h].append(start(piece, piece, along(h, d)))
        over.append(start(piece, piece, sibling))
    for d in (1, 3, 2):
        for h in range(2):
            wide[h][d - 1].wait_recv()
            piece = chunk(h, lax.rem(me[h] + 4 - d, 4))
            over.append(start(piece, piece, sibling))
    for copy in finish:
        copy.wait()
    own_q.wait()
    qf_ref[...] = qz_ref[...].astype(jnp.float32)
    for copy in over:
        copy.wait()
    for copy in cross + first[0] + first[1] + second[0] + second[1] + there + back + spread[0] + spread[1] + wide[0] + wide[1]:
        copy.wait_send()


def sum_gram(t, queries):
    f32 = jnp.float32
    rows, width = queries.shape
    return pl.pallas_call(
        gram_kernel,
        in_specs=[pl.BlockSpec(memory_space=pl.ANY), pl.BlockSpec(memory_space=pltpu.VMEM)],
        out_specs=[pl.BlockSpec(memory_space=pltpu.VMEM)] * 2,
        out_shape=[
            jax.ShapeDtypeStruct((2 * HALF, BLK), f32),
            jax.ShapeDtypeStruct((8 * rows, width), f32),
        ],
        scratch_shapes=[
            pltpu.VMEM((8 * rows, width), jnp.bfloat16),
            pltpu.VMEM((width // WIDE, t.shape[0], WIDE), jnp.bfloat16),
            pltpu.VMEM((HALF, BLK), f32),
            pltpu.VMEM((HALF, BLK), f32),
            pltpu.VMEM((HALF, BLK), f32),
            pltpu.VMEM((2, 3, 4 * ROWS, BLK), f32),
            pltpu.VMEM((2, 4 * ROWS, BLK), f32),
            pltpu.VMEM((2, 3, ROWS, BLK), f32),
            pltpu.VMEM((8 * ZROWS, BLK), f32),
            pltpu.VMEM((7, ZROWS, BLK), f32),
            pltpu.VMEM((8 * ZROWS, BLK), f32),
            pltpu.SemaphoreType.DMA((4,)),
            pltpu.SemaphoreType.DMA,
            pltpu.SemaphoreType.DMA((64,)),
            pltpu.SemaphoreType.DMA((64,)),
        ],
        compiler_params=pltpu.CompilerParams(collective_id=0, has_side_effects=True, vmem_limit_bytes=56 * 1024 * 1024),
        name="sum_gram",
    )(t, queries)


def split(v):
    hi = v.astype(jnp.bfloat16)
    return hi, (v - hi.astype(jnp.float32)).astype(jnp.bfloat16)


def store_kernel(sol_ref, out_ref):
    rows, width = sol_ref.shape
    for h in range(2):
        part = sol_ref[:, h * (width // 2):(h + 1) * (width // 2)]
        out_ref[h * rows:(h + 1) * rows, :] = part.astype(jnp.bfloat16)


def solve_kernel(total, most, g_ref, q_ref, out_ref, flag_ref, hi_ref, lo_ref, d_ref):
    rows, width = q_ref.shape
    eye = lax.broadcasted_iota(jnp.int32, (BLK, BLK), 0) == lax.broadcasted_iota(jnp.int32, (BLK, BLK), 1)
    square = jnp.zeros((BLK, BLK), jnp.float32)
    for i, j in PAIRS:
        at = SLOT[i, j] * BLK
        block = g_ref[at:at + BLK, :] * (1.0 / total)
        if i == j:
            d_ref[:, i * BLK:(i + 1) * BLK] = jnp.sum(jnp.where(eye, block, 0.0), axis=0, keepdims=True) + DAMP
            block = jnp.where(eye, 0.0, block)
            square += block * block
        else:
            square += 2.0 * block * block
        hi, lo = split(block)
        hi_ref[i * BLK:(i + 1) * BLK, j * BLK:(j + 1) * BLK] = hi
        lo_ref[i * BLK:(i + 1) * BLK, j * BLK:(j + 1) * BLK] = lo
        if i != j:
            hi, lo = split(block.T)
            hi_ref[j * BLK:(j + 1) * BLK, i * BLK:(i + 1) * BLK] = hi
            lo_ref[j * BLK:(j + 1) * BLK, i * BLK:(i + 1) * BLK] = lo
    size = jnp.sum(square)
    diag = d_ref[...]

    def apply(v):
        hi, lo = split(v)
        both = jnp.dot(jnp.concatenate([hi, lo], axis=0), hi_ref[...], preferred_element_type=jnp.float32)
        low = jnp.dot(hi, lo_ref[...], preferred_element_type=jnp.float32)
        return v * diag + (both[:rows] + (both[rows:] + low))

    def dots(a, b):
        return jnp.sum(a * b, axis=1, keepdims=True)

    def unsolved(state):
        step, _, _, _, _, left = state
        return jnp.logical_and(step < most, left > 0.0)

    def advance(state):
        step, sol, res, way, rr, _ = state
        image = apply(way)
        bend = dots(way, image)
        alpha = jnp.where(bend > 0.0, rr / bend, 0.0)
        sol = sol + alpha * way
        res = res - alpha * image
        after = dots(res, res)
        beta = jnp.where(rr > 0.0, after / rr, 0.0)
        left = jnp.sum(jnp.where(after <= (DAMP * TAU) ** 2 * dots(sol, sol), 0.0, 1.0))
        return step + 1, sol, res, res + beta * way, after, left

    res = q_ref[...]
    state = (jnp.int32(0), jnp.zeros((rows, width), jnp.float32), res, res, dots(res, res), jnp.float32(1.0))
    _, sol, _, _, _, left = lax.while_loop(unsolved, advance, state)
    for h in range(2):
        out_ref[h * rows:(h + 1) * rows, :] = sol[:, h * (width // 2):(h + 1) * (width // 2)].astype(jnp.bfloat16)
    good = jnp.logical_and(left == 0.0, size <= 4.0)
    flag_ref[0, 0] = jnp.where(good, 1, 0).astype(jnp.int32)


def solve(packed, queries, total):
    rows, width = queries.shape
    return pl.pallas_call(
        functools.partial(solve_kernel, total, 48),
        in_specs=[pl.BlockSpec(memory_space=pltpu.VMEM)] * 2,
        out_specs=[pl.BlockSpec(memory_space=pltpu.VMEM), pl.BlockSpec(memory_space=pltpu.SMEM)],
        out_shape=[
            jax.ShapeDtypeStruct((2 * rows, width // 2), jnp.bfloat16),
            jax.ShapeDtypeStruct((1, 1), jnp.int32),
        ],
        scratch_shapes=[
            pltpu.VMEM((width, width), jnp.bfloat16),
            pltpu.VMEM((width, width), jnp.bfloat16),
            pltpu.VMEM((1, width), jnp.float32),
        ],
        compiler_params=pltpu.CompilerParams(vmem_limit_bytes=24 * 1024 * 1024),
        name="solve_rows",
    )(packed, queries)


def solve_direct(packed, queries, total):
    rows, width = queries.shape
    blocks = packed.reshape(len(PAIRS), BLK, BLK)
    bands = []
    for i in range(NB):
        row = [blocks[SLOT[i, j]] if i >= j else blocks[SLOT[j, i]].T for j in range(NB)]
        bands.append(jnp.concatenate(row, axis=1))
    fisher = jnp.concatenate(bands, axis=0) / total + DAMP * jnp.eye(width, dtype=jnp.float32)
    factor = jnp.linalg.cholesky(fisher)
    half = lax.linalg.triangular_solve(
        factor, queries, left_side=False, lower=True, transpose_a=True
    )
    solved = lax.linalg.triangular_solve(factor, half, left_side=False, lower=True)
    return pl.pallas_call(
        store_kernel,
        in_specs=[pl.BlockSpec(memory_space=pltpu.VMEM)],
        out_specs=pl.BlockSpec(memory_space=pltpu.VMEM),
        out_shape=jax.ShapeDtypeStruct((2 * rows, width // 2), jnp.bfloat16),
        name="store_rows",
    )(solved)


def gather_kernel(p_ref, out_ref, own_sem, send, recv):
    core, x, y, z = coords()
    sibling = device(1 - core, x, y, z)

    def along(axis, d):
        if axis == 0:
            return device(core, lax.rem(x + d, 4), y, z)
        return device(core, x, lax.rem(y + d, 4), z)

    own = [pltpu.make_async_copy(p_ref.at[h], out_ref.at[h, x, :, y, core], own_sem.at[h]) for h in range(2)]
    for copy in own:
        copy.start()
    peers = [sibling] + [along(a, d) for a in (0, 1) for d in (1, 3)]
    barrier = pltpu.get_barrier_semaphore()
    for peer in peers:
        pl.semaphore_signal(barrier, inc=1, device_id=peer, device_id_type=MESH)
    pl.semaphore_wait(barrier, len(peers))
    count = [0]
    sent = []

    def start(piece, to, src=None):
        n = count[0]
        count[0] += 1
        copy = pltpu.make_async_remote_copy(
            src_ref=piece if src is None else src,
            dst_ref=piece,
            send_sem=send.at[n],
            recv_sem=recv.at[n],
            device_id=to,
            device_id_type=MESH,
        )
        copy.start()
        sent.append(copy)
        return copy

    whole, low, high = pl.ds(0, 8), pl.ds(0, 4), pl.ds(4, 4)

    def piece(h, da, db, zs=whole):
        if h == 0:
            return out_ref.at[0, lax.rem(x + da, 4), zs, lax.rem(y + db, 4), core]
        return out_ref.at[1, lax.rem(x + db, 4), zs, lax.rem(y + da, 4), core]

    both = range(2)
    over = []
    near = [[start(piece(h, 0, 0), along(1 - h, d), p_ref.at[h]) for d in (1, 3)] for h in both]
    far = [{}, {}]

    def first(h, db, src=None):
        far[h][db] = [start(piece(h, 0, db), along(h, d), src) for d in (1, 3)]

    def hand(h, da, db):
        over.append(start(piece(h, da, db), sibling))

    for h in both:
        first(h, 0, p_ref.at[h])
        over.append(start(piece(h, 0, 0), sibling, p_ref.at[h]))
    opposite = []
    for h in both:
        for copy in near[h]:
            copy.wait_recv()
        opposite.append([
            start(piece(h, 0, 3, low), along(1 - h, 1)),
            start(piece(h, 0, 1, high), along(1 - h, 3)),
        ])
        for db in (3, 1):
            first(h, db)
            hand(h, 0, db)
    last = []

    def forward(h, db):
        for copy in far[h][db]:
            copy.wait_recv()
        last.append((h, db, start(piece(h, 3, db, low), along(h, 1)), start(piece(h, 1, db, high), along(h, 3))))
        hand(h, 3, db)
        hand(h, 1, db)

    for h in both:
        forward(h, 0)
    for h in both:
        for copy in opposite[h]:
            copy.wait_recv()
        first(h, 2)
        hand(h, 0, 2)
    for db in (3, 1, 2):
        for h in both:
            forward(h, db)
    for h, db, up, down in last:
        up.wait_recv()
        down.wait_recv()
        hand(h, 2, db)
    for copy in over:
        copy.wait_recv()
    for copy in own:
        copy.wait()
    for copy in sent:
        copy.wait_send()


def gather_queries(precond):
    zs, rows, width = 8, precond.shape[0] // 16, precond.shape[1]
    out = pl.pallas_call(
        gather_kernel,
        in_specs=[pl.BlockSpec(memory_space=pltpu.VMEM)],
        out_specs=pl.BlockSpec(memory_space=pltpu.VMEM),
        out_shape=jax.ShapeDtypeStruct((2, 4, zs, 4, 2, rows, width), jnp.bfloat16),
        scratch_shapes=[
            pltpu.SemaphoreType.DMA((2,)),
            pltpu.SemaphoreType.DMA((80,)),
            pltpu.SemaphoreType.DMA((80,)),
        ],
        compiler_params=pltpu.CompilerParams(collective_id=1, has_side_effects=True, vmem_limit_bytes=16 * 1024 * 1024),
        name="gather_queries",
    )(precond.reshape(2, zs, rows, width))
    return out.reshape(2, 32, QROWS, width)


PER = 4


def score_kernel(scale, pair_ref, count_ref, t_ref, p_ref, out_ref):
    step = pl.program_id(0)
    half = t_ref.shape[1] // 2
    slots = out_ref.shape[1]
    nt = (((1,), (1,)), ((), ()))
    for i in range(PER):
        b = step * PER + i
        grads = t_ref[i * TRB:(i + 1) * TRB, :]
        chosen = [pair_ref[s, b] for s in range(slots)]
        value = 0.0
        for h in range(2):
            tasks = jnp.concatenate([p_ref[h, q] for q in chosen], axis=0)
            value += lax.dot_general(
                grads[:, h * half:(h + 1) * half], tasks, nt, preferred_element_type=jnp.float32
            )
        value *= scale
        for s in range(slots):
            live = s < count_ref[b]
            part = value[:, s * QROWS:(s + 1) * QROWS]
            out_ref[i, s] = jnp.where(live, part, 0.0).astype(out_ref.dtype)


def score(t, queries, pair_blocks, counts):
    blocks, slots = pair_blocks.shape
    width = t.shape[1]
    return pl.pallas_call(
        functools.partial(score_kernel, 1.0 / math.sqrt(width)),
        grid_spec=pltpu.PrefetchScalarGridSpec(
            num_scalar_prefetch=2,
            grid=(blocks // PER,),
            in_specs=[
                pl.BlockSpec((PER * TRB, width), lambda b, *_: (b, 0)),
                pl.BlockSpec(memory_space=pltpu.VMEM),
            ],
            out_specs=pl.BlockSpec((PER, slots, TRB, QROWS), lambda b, *_: (b, 0, 0, 0)),
        ),
        out_shape=jax.ShapeDtypeStruct((blocks, slots, TRB, QROWS), jnp.bfloat16),
        compiler_params=pltpu.CompilerParams(vmem_limit_bytes=32 * 1024 * 1024),
        name="scores",
    )(pair_blocks.T, counts, t, queries)


def per_device(train_grads, queries, pair_blocks, counts):
    total = lax.axis_size("train") * lax.axis_size("task") * train_grads.shape[0]
    packed, queries = sum_gram(train_grads, queries)
    precond, flag = solve(packed, queries, total)
    precond = lax.cond(
        flag[0, 0] > 0,
        lambda p, g, q: p,
        lambda p, g, q: solve_direct(g, q, total),
        precond, packed, queries,
    )
    return score(train_grads, gather_queries(precond), pair_blocks, counts)


def solution(mesh):
    in_specs = (
        P(("train", "task"), None),
        P(("task", "train"), None),
        P(("train", "task"), None),
        P(("train", "task")),
    )
    out_specs = P(("train", "task"), None, None, None)
    return jax.shard_map(
        per_device, mesh=mesh, in_specs=in_specs, out_specs=out_specs, check_vma=False
    )
```

```python
import functools
import math

import jax
import jax.numpy as jnp
from jax import lax
from jax.experimental import pallas as pl
from jax.experimental.pallas import tpu as pltpu
from jax.sharding import PartitionSpec as P

MESH = pl.DeviceIdType.MESH
TRB = 256
QROWS = 128
BLK = 128
NB = 8
DAMP = 0.1
TAU = 1e-4
WIDE = 256


def coords():
    t, k = lax.axis_index("train"), lax.axis_index("task")
    core, y, x = lax.rem(t, 2), lax.rem(t // 2, 4), k // 2
    z = lax.rem(k, 2) * 4 + t // 8
    return core, x, y, z


def device(core, x, y, z):
    return ((lax.rem(z, 4) * 4 + y) * 2 + core, x * 2 + z // 4)


STEP = 2 * WIDE
HALF = 5 * STEP
BATCHES = (range(0, 3), range(3, 5))
SLICE = tuple(len(batch) * STEP // 32 for batch in BATCHES)
ZROWS = (16, 8)


def wide_blocks(c):
    return [(2 * c, 2 * c), (2 * c + 1, 2 * c + 1), (2 * c + 1, 2 * c), (2 + c, 1 - c), (2 + c, c)]


PAIRS = [
    (2 * i + u, 2 * j + v) for c in (0, 1) for i, j in wide_blocks(c) for u in range(2) for v in range(2)
]
SLOT = {pair: n for n, pair in enumerate(PAIRS)}


def gram_kernel(t_ref, q_ref, out_ref, qf_ref, tv, qz_ref, gs, r0, s1, *rest):
    ra, s2, rb, s3, rz, fz = (rest[2 * n:2 * n + 2] for n in range(6))
    t_sem, q_sem, send, recv = rest[12:]
    core, x, y, z = coords()
    other = 1 - core
    sibling = device(other, x, y, z)
    me = (x, y)
    both = range(2)

    def along(axis, d):
        if axis == 0:
            return device(core, lax.rem(x + d, 4), y, z)
        if axis == 1:
            return device(core, x, lax.rem(y + d, 4), z)
        return device(core, x, y, lax.rem(z + d, 8))

    loads = []
    for n, panel in enumerate((2 * other, 2 * other + 1, 2 * core, 2 * core + 1)):
        column = pl.multiple_of(panel * WIDE, WIDE)
        loads.append(pltpu.make_async_copy(t_ref.at[:, pl.ds(column, WIDE)], tv.at[panel], t_sem.at[n]))
        loads[n].start()
    place = pl.ds(pl.multiple_of(z * q_ref.shape[0], 16), q_ref.shape[0])
    own_q = pltpu.make_async_copy(q_ref, qz_ref.at[place], q_sem)
    own_q.start()
    peers = [sibling] + [along(a, d) for a in (0, 1) for d in (1, 2, 3)] + [along(2, d) for d in range(1, 8)]
    barrier = pltpu.get_barrier_semaphore()
    for peer in peers:
        pl.semaphore_signal(barrier, inc=1, device_id=peer, device_id_type=MESH)
    sent = []

    def start(src, dst, to):
        n = len(sent)
        copy = pltpu.make_async_remote_copy(
            src_ref=src, dst_ref=dst, send_sem=send.at[n], recv_sem=recv.at[n], device_id=to, device_id_type=MESH
        )
        copy.start()
        sent.append(copy)
        return copy

    def arrive(copies):
        for copy in copies:
            copy.wait_recv()

    def rows(at, length):
        return pl.ds(pl.multiple_of(at, 8), length)

    def block(n, owner):
        i, j = wide_blocks(owner)[n]
        return lax.dot_general(tv[i], tv[j], (((0,), (0,)), ((), ())), preferred_element_type=jnp.float32)

    def quarters(n, value):
        for p in range(4):
            u, v = p // 2, p % 2
            yield n * STEP + p * BLK, value[u * BLK:(u + 1) * BLK, v * BLK:(v + 1) * BLK]

    cross = [None] * 5

    def for_sibling(n):
        value = block(n, other)
        for at, part in quarters(n, value):
            gs[at:at + BLK, :] = part

    def to_sibling(n):
        span = pl.ds(n * STEP, STEP)
        cross[n] = start(gs.at[span], r0.at[span], sibling)

    def for_me(n):
        value = block(n, core)
        for at, part in quarters(n, value):
            s1[at:at + BLK, :] = part

    def join(n):
        cross[n].wait_recv()
        s1[n * STEP:(n + 1) * STEP, :] += r0[n * STEP:(n + 1) * STEP, :]

    def span(k, h, a):
        return BATCHES[k][0] * STEP + (h * 4 + a) * 4 * SLICE[k]

    def first_sends(k):
        size = 4 * SLICE[k]
        return [
            start(s1.at[rows(span(k, h, lax.rem(me[h] + d, 4)), size)], ra[k].at[h, d - 1], along(h, d))
            for d in (2, 1, 3) for h in both
        ]

    for n in range(5):
        if n != 2:
            loads[n - 1 if n > 2 else n].wait()
        for_sibling(n)
    for n in BATCHES[0]:
        for_me(n)
    pl.semaphore_wait(barrier, len(peers))
    for n in range(5):
        to_sibling(n)
    shared = [start(q_ref, qz_ref.at[place], along(2, d)) for d in (4, 3, 5, 2, 6, 1, 7)]
    for n in BATCHES[1]:
        for_me(n)
    first = [None, None]
    for k in both:
        for n in BATCHES[k]:
            join(n)
        first[k] = first_sends(k)
    second, there, back, spread, wide = ([None, None] for _ in range(5))
    for k in both:
        size = SLICE[k]
        arrive(first[k])
        second[k] = []
        for h in both:
            s2[k][h] = s1[rows(span(k, h, me[h]), 4 * size), :] + ra[k][h, 0] + ra[k][h, 1] + ra[k][h, 2]
            for d in (2, 1, 3):
                at = lax.rem(me[1 - h] + d, 4) * size
                second[k].append(start(s2[k].at[h, rows(at, size)], rb[k].at[h, d - 1], along(1 - h, d)))
    for k in both:
        size = SLICE[k]
        if 8 * ZROWS[k] > 2 * size:
            s3[k][2 * size:, :] = jnp.zeros((8 * ZROWS[k] - 2 * size, BLK), jnp.float32)
        arrive(second[k])
        for h in both:
            own = s2[k][h, rows(me[1 - h] * size, size), :]
            s3[k][h * size:(h + 1) * size, :] = own + rb[k][h, 0] + rb[k][h, 1] + rb[k][h, 2]
        there[k] = []
        for d in (4, 3, 5, 2, 6, 1, 7):
            at = lax.rem(z + d, 8) * ZROWS[k]
            there[k].append(start(s3[k].at[rows(at, ZROWS[k])], rz[k].at[d - 1], along(2, d)))
    for k in both:
        mine = rows(z * ZROWS[k], ZROWS[k])
        arrive(there[k])
        total = s3[k][mine, :]
        for d in range(7):
            total += rz[k][d]
        fz[k][mine, :] = total
        back[k] = [start(fz[k].at[mine], fz[k].at[mine], along(2, d)) for d in (4, 3, 5, 2, 6, 1, 7)]
    base = core * HALF

    def chunk(k, h, a):
        return out_ref.at[rows(base + span(k, h, a), 4 * SLICE[k])]

    for k in both:
        size = SLICE[k]
        arrive(back[k])
        spread[k] = []
        for h in both:
            at = rows(base + span(k, h, me[h]) + me[1 - h] * size, size)
            out_ref[at, :] = fz[k][h * size:(h + 1) * size, :]
            spread[k] += [start(out_ref.at[at], out_ref.at[at], along(1 - h, d)) for d in (2, 1, 3)]
    over = []
    for k in both:
        arrive(spread[k])
        wide[k] = []
        for d in (2, 1, 3):
            for h in both:
                piece = chunk(k, h, me[h])
                wide[k].append((d, h, start(piece, piece, along(h, d))))
        for h in both:
            piece = chunk(k, h, me[h])
            over.append(start(piece, piece, sibling))
    arrive(shared)
    own_q.wait()
    qf_ref[...] = qz_ref[...].astype(jnp.float32)
    for k in both:
        for d, h, copy in wide[k]:
            copy.wait_recv()
            piece = chunk(k, h, lax.rem(me[h] + 4 - d, 4))
            over.append(start(piece, piece, sibling))
    arrive(over)
    for copy in sent:
        copy.wait_send()


def sum_gram(t, queries):
    f32 = jnp.float32
    rows, width = queries.shape
    pairs = [
        [(2, 3, 4 * size, BLK) for size in SLICE],
        [(2, 4 * size, BLK) for size in SLICE],
        [(2, 3, size, BLK) for size in SLICE],
        [(8 * size, BLK) for size in ZROWS],
        [(7, size, BLK) for size in ZROWS],
        [(8 * size, BLK) for size in ZROWS],
    ]
    copies = 5 + 7 + 2 * (6 + 6 + 7 + 7 + 6 + 6 + 8)
    return pl.pallas_call(
        gram_kernel,
        in_specs=[pl.BlockSpec(memory_space=pltpu.HBM)] * 2,
        out_specs=[pl.BlockSpec(memory_space=pltpu.VMEM)] * 3,
        out_shape=[
            jax.ShapeDtypeStruct((2 * HALF, BLK), f32),
            jax.ShapeDtypeStruct((8 * rows, width), f32),
            jax.ShapeDtypeStruct((width // WIDE, t.shape[0], WIDE), jnp.bfloat16),
        ],
        scratch_shapes=[pltpu.VMEM((8 * rows, width), jnp.bfloat16)]
        + [pltpu.VMEM((HALF, BLK), f32)] * 3
        + [pltpu.VMEM(shape, f32) for pair in pairs for shape in pair]
        + [
            pltpu.SemaphoreType.DMA((4,)),
            pltpu.SemaphoreType.DMA,
            pltpu.SemaphoreType.DMA((copies,)),
            pltpu.SemaphoreType.DMA((copies,)),
        ],
        compiler_params=pltpu.CompilerParams(
            collective_id=0, has_side_effects=True, vmem_limit_bytes=46 * 1024 * 1024
        ),
        name="sum_gram",
    )(t, queries)


def split(v):
    hi = v.astype(jnp.bfloat16)
    return hi, (v - hi.astype(jnp.float32)).astype(jnp.bfloat16)


def store_kernel(sol_ref, out_ref):
    rows, width = sol_ref.shape
    for h in range(2):
        part = sol_ref[:, h * (width // 2):(h + 1) * (width // 2)]
        out_ref[h * rows:(h + 1) * rows, :] = part.astype(jnp.bfloat16)


def solve_kernel(total, most, g_ref, q_ref, out_ref, flag_ref, hi_ref, lo_ref, d_ref):
    rows, width = q_ref.shape
    eye = lax.broadcasted_iota(jnp.int32, (BLK, BLK), 0) == lax.broadcasted_iota(jnp.int32, (BLK, BLK), 1)
    square = jnp.zeros((BLK, BLK), jnp.float32)
    for i, j in PAIRS:
        if i < j:
            continue
        at = SLOT[i, j] * BLK
        block = g_ref[at:at + BLK, :] * (1.0 / total)
        if i == j:
            d_ref[:, i * BLK:(i + 1) * BLK] = jnp.sum(jnp.where(eye, block, 0.0), axis=0, keepdims=True) + DAMP
            block = jnp.where(eye, 0.0, block)
            square += block * block
        else:
            square += 2.0 * block * block
        hi, lo = split(block)
        hi_ref[i * BLK:(i + 1) * BLK, j * BLK:(j + 1) * BLK] = hi
        lo_ref[i * BLK:(i + 1) * BLK, j * BLK:(j + 1) * BLK] = lo
        if i != j:
            hi, lo = split(block.T)
            hi_ref[j * BLK:(j + 1) * BLK, i * BLK:(i + 1) * BLK] = hi
            lo_ref[j * BLK:(j + 1) * BLK, i * BLK:(i + 1) * BLK] = lo
    size = jnp.sum(square)
    diag = d_ref[...]

    def apply(v):
        hi, lo = split(v)
        both = jnp.dot(jnp.concatenate([hi, lo], axis=0), hi_ref[...], preferred_element_type=jnp.float32)
        low = jnp.dot(hi, lo_ref[...], preferred_element_type=jnp.float32)
        return v * diag + (both[:rows] + (both[rows:] + low))

    def dots(a, b):
        return jnp.sum(a * b, axis=1, keepdims=True)

    def rough(v):
        return v * diag + jnp.dot(v.astype(jnp.bfloat16), hi_ref[...], preferred_element_type=jnp.float32)

    def unsolved(square_norm, sol, tau):
        return jnp.sum(jnp.where(square_norm <= (DAMP * tau) ** 2 * dots(sol, sol), 0.0, 1.0))

    def advance(image, sol, res, way, rr):
        bend = dots(way, image)
        alpha = jnp.where(bend > 0.0, rr / bend, 0.0)
        sol = sol + alpha * way
        res = res - alpha * image
        after = dots(res, res)
        beta = jnp.where(rr > 0.0, after / rr, 0.0)
        return sol, res, res + beta * way, after, unsolved(after, sol, 0.5 * TAU)

    def going(state):
        return jnp.logical_and(state[0] < most, state[-1] > 0.0)

    def step(state):
        return (state[0] + 1,) + advance(rough(state[3]), *state[1:5])

    def check(sol):
        res = queries - apply(sol)
        return res, unsolved(dots(res, res), sol, TAU)

    def again(state):
        turn, sol, res, _ = state
        rr = dots(res, res)
        sol = lax.while_loop(going, step, (jnp.int32(0), sol, res, res, rr, jnp.float32(1.0)))[1]
        return (turn + 1, sol) + check(sol)

    queries = q_ref[...]
    exact = queries.astype(jnp.bfloat16)
    image = queries * diag + (
        jnp.dot(exact, hi_ref[...], preferred_element_type=jnp.float32)
        + jnp.dot(exact, lo_ref[...], preferred_element_type=jnp.float32)
    )
    begin = advance(image, jnp.zeros((rows, width), jnp.float32), queries, queries, dots(queries, queries))
    sol = lax.while_loop(going, step, (jnp.int32(1),) + begin)[1]
    state = (jnp.int32(0), sol) + check(sol)
    _, sol, _, left = lax.while_loop(lambda now: jnp.logical_and(now[0] < 8, now[-1] > 0.0), again, state)
    for h in range(2):
        out_ref[h * rows:(h + 1) * rows, :] = sol[:, h * (width // 2):(h + 1) * (width // 2)].astype(jnp.bfloat16)
    good = jnp.logical_and(left == 0.0, size <= 4.0)
    flag_ref[0, 0] = jnp.where(good, 1, 0).astype(jnp.int32)


def solve(packed, queries, total):
    rows, width = queries.shape
    return pl.pallas_call(
        functools.partial(solve_kernel, total, 48),
        in_specs=[pl.BlockSpec(memory_space=pltpu.VMEM)] * 2,
        out_specs=[pl.BlockSpec(memory_space=pltpu.VMEM), pl.BlockSpec(memory_space=pltpu.SMEM)],
        out_shape=[
            jax.ShapeDtypeStruct((2 * rows, width // 2), jnp.bfloat16),
            jax.ShapeDtypeStruct((1, 1), jnp.int32),
        ],
        scratch_shapes=[
            pltpu.VMEM((width, width), jnp.bfloat16),
            pltpu.VMEM((width, width), jnp.bfloat16),
            pltpu.VMEM((1, width), jnp.float32),
        ],
        compiler_params=pltpu.CompilerParams(vmem_limit_bytes=24 * 1024 * 1024),
        name="solve_rows",
    )(packed, queries)


def solve_direct(packed, queries, total):
    rows, width = queries.shape
    blocks = packed.reshape(len(PAIRS), BLK, BLK)
    bands = []
    for i in range(NB):
        row = [blocks[SLOT[i, j]] if i >= j else blocks[SLOT[j, i]].T for j in range(NB)]
        bands.append(jnp.concatenate(row, axis=1))
    fisher = jnp.concatenate(bands, axis=0) / total + DAMP * jnp.eye(width, dtype=jnp.float32)
    factor = jnp.linalg.cholesky(fisher)
    half = lax.linalg.triangular_solve(
        factor, queries, left_side=False, lower=True, transpose_a=True
    )
    solved = lax.linalg.triangular_solve(factor, half, left_side=False, lower=True)
    return pl.pallas_call(
        store_kernel,
        in_specs=[pl.BlockSpec(memory_space=pltpu.VMEM)],
        out_specs=pl.BlockSpec(memory_space=pltpu.VMEM),
        out_shape=jax.ShapeDtypeStruct((2 * rows, width // 2), jnp.bfloat16),
        name="store_rows",
    )(solved)


def gather_kernel(p_ref, out_ref, own_sem, send, recv):
    core, x, y, z = coords()
    sibling = device(1 - core, x, y, z)

    def along(axis, d):
        if axis == 0:
            return device(core, lax.rem(x + d, 4), y, z)
        return device(core, x, lax.rem(y + d, 4), z)

    own = [pltpu.make_async_copy(p_ref.at[h], out_ref.at[h, x, :, y, core], own_sem.at[h]) for h in range(2)]
    for copy in own:
        copy.start()
    peers = [sibling] + [along(a, d) for a in (0, 1) for d in (1, 3)]
    barrier = pltpu.get_barrier_semaphore()
    for peer in peers:
        pl.semaphore_signal(barrier, inc=1, device_id=peer, device_id_type=MESH)
    pl.semaphore_wait(barrier, len(peers))
    count = [0]

    def start(piece, to, src=None):
        n = count[0]
        count[0] += 1
        copy = pltpu.make_async_remote_copy(
            src_ref=piece if src is None else src,
            dst_ref=piece,
            send_sem=send.at[n],
            recv_sem=recv.at[n],
            device_id=to,
            device_id_type=MESH,
        )
        copy.start()
        return copy

    whole, low, high = pl.ds(0, 8), pl.ds(0, 4), pl.ds(4, 4)

    def piece(h, da, db, zs=whole):
        if h == 0:
            return out_ref.at[0, lax.rem(x + da, 4), zs, lax.rem(y + db, 4), core]
        return out_ref.at[1, lax.rem(x + db, 4), zs, lax.rem(y + da, 4), core]

    both = range(2)
    over, rounds = [], []

    def launch(copies):
        rounds.append(copies)
        if len(rounds) > 2:
            for copy in rounds[-3]:
                copy.wait_send()

    def hand(h, da, db, src=None):
        over.append(start(piece(h, da, db), sibling, src))

    far = {}

    def first(db, own=False):
        far[db] = [[start(piece(h, 0, db), along(h, d), p_ref.at[h] if own else None) for d in (1, 3)] for h in both]
        launch(far[db][0] + far[db][1])

    last = []

    def forward(db):
        group = []
        for h in both:
            for copy in far[db][h]:
                copy.wait_recv()
            pair = [start(piece(h, 3, db, low), along(h, 1)), start(piece(h, 1, db, high), along(h, 3))]
            last.append((h, db, pair))
            group += pair
        launch(group)
        for h in both:
            hand(h, 3, db)
            hand(h, 1, db)

    near = [[start(piece(h, 0, 0), along(1 - h, d), p_ref.at[h]) for d in (1, 3)] for h in both]
    launch(near[0] + near[1])
    for h in both:
        hand(h, 0, 0, p_ref.at[h])
    first(0, True)
    opposite = []
    for h in both:
        for copy in near[h]:
            copy.wait_recv()
        opposite += [start(piece(h, 0, 3, low), along(1 - h, 1)), start(piece(h, 0, 1, high), along(1 - h, 3))]
    launch(opposite)
    for h in both:
        for db in (3, 1):
            hand(h, 0, db)
    first(3)
    first(1)
    forward(0)
    for copy in opposite:
        copy.wait_recv()
    first(2)
    for h in both:
        hand(h, 0, 2)
    for db in (3, 1, 2):
        forward(db)
    for h, db, pair in last:
        for copy in pair:
            copy.wait_recv()
        hand(h, 2, db)
    for copy in over:
        copy.wait_recv()
    for copy in own:
        copy.wait()
    for copy in over + rounds[-2] + rounds[-1]:
        copy.wait_send()


def gather_queries(precond):
    zs, rows, width = 8, precond.shape[0] // 16, precond.shape[1]
    out = pl.pallas_call(
        gather_kernel,
        in_specs=[pl.BlockSpec(memory_space=pltpu.VMEM)],
        out_specs=pl.BlockSpec(memory_space=pltpu.VMEM),
        out_shape=jax.ShapeDtypeStruct((2, 4, zs, 4, 2, rows, width), jnp.bfloat16),
        scratch_shapes=[
            pltpu.SemaphoreType.DMA((2,)),
            pltpu.SemaphoreType.DMA((80,)),
            pltpu.SemaphoreType.DMA((80,)),
        ],
        compiler_params=pltpu.CompilerParams(collective_id=1, has_side_effects=True, vmem_limit_bytes=16 * 1024 * 1024),
        name="gather_queries",
    )(precond.reshape(2, zs, rows, width))
    return out.reshape(2, 32, QROWS, width)


PER = 4


def score_kernel(scale, pair_ref, count_ref, t_ref, p_ref, out_ref):
    step = pl.program_id(0)
    slots = out_ref.shape[1]
    for i in range(PER):
        b = step * PER + i
        rows = pl.ds(pl.multiple_of(b * TRB, TRB), TRB)
        grads = jnp.concatenate([t_ref[n, rows, :] for n in range(t_ref.shape[0])], axis=1)
        chosen = [pair_ref[s, b] for s in range(slots)]
        tasks = jnp.concatenate([jnp.concatenate([p_ref[h, q] for q in chosen], axis=0) for h in range(2)], axis=1)
        value = lax.dot_general(grads, tasks, (((1,), (1,)), ((), ())), preferred_element_type=jnp.float32) * scale
        for s in range(slots):
            live = s < count_ref[b]
            part = value[:, s * QROWS:(s + 1) * QROWS]
            out_ref[i, s] = jnp.where(live, part, 0.0).astype(out_ref.dtype)


def score(panels, queries, pair_blocks, counts):
    blocks, slots = pair_blocks.shape
    width = panels.shape[0] * panels.shape[2]
    return pl.pallas_call(
        functools.partial(score_kernel, 1.0 / math.sqrt(width)),
        grid_spec=pltpu.PrefetchScalarGridSpec(
            num_scalar_prefetch=2,
            grid=(blocks // PER,),
            in_specs=[pl.BlockSpec(memory_space=pltpu.VMEM)] * 2,
            out_specs=pl.BlockSpec((PER, slots, TRB, QROWS), lambda b, *_: (b, 0, 0, 0)),
        ),
        out_shape=jax.ShapeDtypeStruct((blocks, slots, TRB, QROWS), jnp.bfloat16),
        compiler_params=pltpu.CompilerParams(vmem_limit_bytes=32 * 1024 * 1024),
        name="scores",
    )(pair_blocks.T, counts, panels, queries)


def per_device(train_grads, queries, pair_blocks, counts):
    total = lax.axis_size("train") * lax.axis_size("task") * train_grads.shape[0]
    packed, queries, panels = sum_gram(train_grads, queries)
    precond, flag = solve(packed, queries, total)
    precond = lax.cond(
        flag[0, 0] > 0,
        lambda p, g, q: p,
        lambda p, g, q: solve_direct(g, q, total),
        precond, packed, queries,
    )
    return score(panels, gather_queries(precond), pair_blocks, counts)


def solution(mesh):
    in_specs = (
        P(("train", "task"), None),
        P(("task", "train"), None),
        P(("train", "task"), None),
        P(("train", "task")),
    )
    out_specs = P(("train", "task"), None, None, None)
    return jax.shard_map(
        per_device, mesh=mesh, in_specs=in_specs, out_specs=out_specs, check_vma=False
    )
```
